256 devices in a mesh: rows: 64 (over z, x, core), cols: 4 (over y).
Axes of the slice: x: 4, y: 4, z: 8, core: 2. Of those that a mesh axis runs over, the one named last changes fastest.
Arguments:
- activations: bfloat16 [131072, 8192], P('rows', 'cols'), may hold values from -120 to 120
- sketch: bfloat16 [8192, 256], P('cols'), may hold values from -0.0625 to 0.0625
Outputs:
- basis: bfloat16 [131072, 256], P(('rows', 'cols'))
- projected: float32 [256, 8192], P(None, 'cols')
The draws below stay inside these ranges and needn't reach their ends.
All inputs are finite; a program needn't handle non-finite values.
Results may differ from the reference program's by a relative error of at most 0.0051.
Values may be sent and summed in bfloat16 or wider, within the bound.
No kernel may reach another device: no remote copies, remote signals or barrier semaphores. Data moves between devices by JAX's collectives and lax.ppermute only.
A program may use at most 64 MiB of HBM per device.

```python
import math
import jax
import jax.numpy as jnp
from jax import lax

D = 8192
RANK = 256
TOKENS = 131072


def draw_activations(key, part):
    key = jax.random.fold_in(key, 5)
    key_base, key_rows, key_cols = jax.random.split(key, 3)
    base_values = jnp.clip(jax.random.normal(key_base, (TOKENS, D), jnp.float32), -6.0, 6.0)
    row_scales = jnp.exp(jax.random.uniform(key_rows, (TOKENS, 1), jnp.float32) * math.log(10.0))
    col_scales = jnp.exp(jax.random.uniform(key_cols, (1, D), jnp.float32, -math.log(2.0), math.log(2.0)))
    return (base_values * row_scales * col_scales).astype(jnp.bfloat16)


def steps_of(key, extent, cuts, least, largest):
    def one(dim, blocks):
        steps = jax.random.uniform(jax.random.fold_in(jax.random.fold_in(key, 6), dim), (blocks,), jnp.float32, least / len(cuts), largest / len(cuts))
        return jnp.repeat(jnp.exp(steps), extent[dim] // blocks).reshape((-1,) + (1,) * (len(extent) - dim - 1))

    loudness = one(*cuts[0])
    for cut in cuts[1:]:
        loudness = loudness * one(*cut)
    return loudness


def gaussian(stream_key, dims, deviation, most, cuts=(), dtype=jnp.bfloat16):
    result = jax.random.normal(stream_key, dims, jnp.float32) * deviation
    if len(cuts) > 0:
        result = steps_of(stream_key, dims, cuts, -0.22, 0.18) * result
    return jnp.clip(result, min=-most, max=most).astype(dtype)


def setup_inputs(seed: int = 0) -> dict:
    splits = jax.random.split(jax.random.key(seed), 3)
    return {
        "activations": draw_activations(jax.random.fold_in(splits[2], 71), 0),
        "sketch": gaussian(splits[1], (D, RANK), D ** -0.5, 0.0625, ((0, 4),)),
    }


def reference(activations, sketch):
    first_image = jnp.dot(activations.astype(jnp.float32), sketch.astype(jnp.float32), preferred_element_type=jnp.float32).astype(jnp.bfloat16)
    back_image = lax.dot_general(activations.astype(jnp.float32), first_image.astype(jnp.float32), (((0,), (0,)), ((), ())), preferred_element_type=jnp.float32).astype(jnp.bfloat16)
    power_image = jnp.dot(activations.astype(jnp.float32), back_image.astype(jnp.float32), preferred_element_type=jnp.float32)
    gram_matrix = jnp.dot(power_image.T.astype(jnp.float32), power_image.astype(jnp.float32), precision=lax.Precision.HIGHEST, preferred_element_type=jnp.float32)
    gram_matrix = gram_matrix / TOKENS
    factor = jnp.linalg.cholesky(gram_matrix)
    solved = jax.scipy.linalg.solve_triangular(factor, power_image.T, lower=True)
    basis = solved.T.astype(jnp.bfloat16)
    projected = lax.dot_general(basis.astype(jnp.float32), activations.astype(jnp.float32), (((0,), (0,)), ((), ())), preferred_element_type=jnp.float32)
    return (basis, projected * (1.0 / math.sqrt(TOKENS)))
```

```python
import math

import jax
import jax.numpy as jnp
from jax import lax
from jax.sharding import PartitionSpec as P

NZ, NX, NC, NY = 8, 4, 2, 4
F32, BF16 = jnp.float32, jnp.bfloat16


def row_index(z, x, c):
    return (z * NX + x) * NC + c


def shift_pairs(axis, k):
    if axis == "y":
        return [(i, (i + k) % NY) for i in range(NY)]
    pairs = []
    for z in range(NZ):
        for x in range(NX):
            for c in range(NC):
                if axis == "x":
                    to = (z, (x + k) % NX, c)
                elif axis == "z":
                    to = ((z + k) % NZ, x, c)
                else:
                    to = (z, x, (c + k) % NC)
                pairs.append((row_index(z, x, c), row_index(*to)))
    return pairs


Z_GROUPS = [[row_index(z, x, c) for z in range(NZ)] for x in range(NX) for c in range(NC)]
SIZE = {"x": NX, "y": NY, "z": NZ, "c": NC}


def shift(value, axis, k):
    return lax.ppermute(value, "cols" if axis == "y" else "rows", shift_pairs(axis, k))


def place(axis):
    if axis == "y":
        return lax.axis_index("cols")
    r = lax.axis_index("rows")
    return {"c": r % NC, "x": (r // NC) % NX, "z": r // (NC * NX)}[axis]


def scatter_sum(part, axis, dtype):
    n, me = SIZE[axis], place(axis)
    m = part.shape[0] // n
    total = lax.dynamic_slice_in_dim(part, me * m, m, 0)
    order = sorted(range(1, n), key=lambda k: -min(k, n - k))
    got = []
    for k in order:
        piece = lax.dynamic_slice_in_dim(part, ((me + k) % n) * m, m, 0)
        got.append(shift(piece.astype(dtype), axis, k))
    for piece in got:
        total = total + piece.astype(F32)
    return total


def gather(mine, axis):
    n, me = SIZE[axis], place(axis)
    m = mine.shape[0]
    order = sorted(range(1, n), key=lambda k: -min(k, n - k))
    got = {k: shift(mine, axis, n - k) for k in order}
    relative = [mine] + [got[k] for k in range(1, n)]
    twice = jnp.concatenate(relative + relative, axis=0)
    return lax.dynamic_slice_in_dim(twice, ((n - me) % n) * m, n * m, 0)


def scatter_sum_z(part, dtype):
    m = part.shape[0] // NZ
    got = lax.all_to_all(part.astype(dtype), "rows", 0, 0, tiled=True, axis_index_groups=Z_GROUPS)
    return jnp.sum(got.reshape(NZ, m, part.shape[1]).astype(F32), axis=0)


def gather_z(mine):
    wide = jnp.concatenate([mine] * NZ, axis=0)
    return lax.all_to_all(wide, "rows", 0, 0, tiled=True, axis_index_groups=Z_GROUPS)


def sum_rows_scattered(part):
    part = scatter_sum(part, "c", BF16)
    part = scatter_sum(part, "x", BF16)
    return scatter_sum_z(part, BF16)


def gather_rows(mine):
    return gather(gather(gather_z(mine), "x"), "c")


def sum_gram(gram):
    gram = scatter_sum(gram, "y", F32)
    gram = gram + shift(gram, "c", 1)
    far, up, down = [shift(gram, "x", k) for k in (2, 1, 3)]
    gram = (gram + far) + (up + down)
    gram = jnp.sum(gather_z(gram).reshape(NZ, *gram.shape), axis=0)
    return gather(gram, "y")


def per_device(activations, sketch):
    token_count = activations.shape[0] * lax.axis_size("rows")
    inverse_root = 1.0 / math.sqrt(token_count)
    product = jnp.dot(activations, sketch, preferred_element_type=F32)
    image = gather(scatter_sum(product, "y", BF16).astype(BF16), "y")
    back = lax.dot_general(
        activations, image, (((0,), (0,)), ((), ())), preferred_element_type=F32
    )
    back_image = gather_rows(sum_rows_scattered(back).astype(BF16))
    product = jnp.dot(activations, back_image, preferred_element_type=F32)
    power = scatter_sum(product, "y", BF16)
    gram = jnp.dot(power.T, power, precision=lax.Precision.HIGHEST, preferred_element_type=F32)
    gram = sum_gram(gram) / token_count
    factor = jnp.linalg.cholesky(gram)
    inverse = jax.scipy.linalg.solve_triangular(factor, jnp.eye(factor.shape[0], dtype=F32), lower=True)
    basis = lax.dot_general(
        power, inverse, (((1,), (1,)), ((), ())),
        precision=lax.Precision.HIGHEST, preferred_element_type=F32,
    ).astype(BF16)
    power_low = gather(power.astype(BF16), "y")
    across = lax.dot_general(
        activations, power_low, (((0,), (0,)), ((), ())), preferred_element_type=F32
    )
    across = gather_rows(sum_rows_scattered(across).astype(BF16))
    projected = lax.dot_general(
        inverse, across.astype(F32), (((1,), (1,)), ((), ())),
        precision=lax.Precision.HIGHEST, preferred_element_type=F32,
    ) * inverse_root
    return (basis, projected)


def solution(mesh):
    placed = (P("rows", "cols"), P("cols", None))
    return jax.shard_map(
        per_device,
        mesh=mesh,
        in_specs=placed,
        out_specs=(P(("rows", "cols"), None), P(None, "cols")),
        check_vma=False,
    )
```

```python
import math

import jax
import jax.numpy as jnp
from jax import lax
from jax.experimental import pallas as pl
from jax.experimental.pallas import tpu as pltpu
from jax.sharding import PartitionSpec as P

NZ, NX, NC, NY = 8, 4, 2, 4
PLANE = NZ * NX
F32, BF16 = jnp.float32, jnp.bfloat16
EXACT = lax.Precision.HIGHEST
FIRST = (((0,), (0,)), ((), ()))
LAST = (((1,), (1,)), ((), ()))
PARAMS = pltpu.CompilerParams(vmem_limit_bytes=48 * 2**20)


def row_index(z, x, c):
    return (z * NX + x) * NC + c


Y_SHIFT = {k: [(i, (i + k) % NY) for i in range(NY)] for k in range(1, NY)}
CORE_SWAP = [(i, i ^ 1) for i in range(NZ * NX * NC)]
PLANES = [[row_index(z, x, c) for z in range(NZ) for x in range(NX)] for c in range(NC)]


def from_y(value, k):
    return lax.ppermute(value, "cols", Y_SHIFT[k])


def from_core(value):
    return lax.ppermute(value, "rows", CORE_SWAP)


def exchange(value):
    return lax.all_to_all(value, "rows", 0, 0, tiled=True, axis_index_groups=PLANES)


def forward_kernel(place, a, b, one, two, three, own):
    step = pl.program_id(0)
    part = jnp.dot(a[...], b[...], preferred_element_type=F32)
    store_quarter(step, part, one, two, three, own)


def forward_halves_kernel(place, a, mine, other, one, two, three, own):
    step = pl.program_id(0)
    half = mine.shape[1]
    here = pl.multiple_of(place[1] * half, half)
    there = pl.multiple_of((1 - place[1]) * half, half)
    part = lax.dot_general(a[:, pl.ds(here, half)], mine[...], LAST, preferred_element_type=F32)
    part += lax.dot_general(a[:, pl.ds(there, half)], other[...], LAST, preferred_element_type=F32)
    store_quarter(step, part, one, two, three, own)


def store_quarter(step, part, one, two, three, own):
    for k, out in enumerate((one, two, three)):
        @pl.when(step == k)
        def _(out=out):
            out[...] = part.astype(BF16)

    @pl.when(step == NY - 1)
    def _():
        own[...] = part


def whole(shape):
    return pl.BlockSpec(shape, lambda s, place: (0,) * len(shape))


def forward(place, activations, *right):
    rows, width = activations.shape
    m, rank = rows // NY, 256
    kernel = forward_kernel if len(right) == 1 else forward_halves_kernel
    return pl.pallas_call(
        kernel,
        grid_spec=pltpu.PrefetchScalarGridSpec(
            num_scalar_prefetch=1,
            grid=(NY,),
            in_specs=[pl.BlockSpec((m, width), lambda s, place: (lax.rem(place[0] + s + 1, NY), 0))]
            + [whole(r.shape) for r in right],
            out_specs=[whole((m, rank))] * NY,
        ),
        out_shape=[jax.ShapeDtypeStruct((m, rank), BF16)] * (NY - 1)
        + [jax.ShapeDtypeStruct((m, rank), F32)],
        compiler_params=PARAMS,
        cost_estimate=pl.CostEstimate(
            flops=2 * rows * width * rank, bytes_accessed=rows * width * 2, transcendentals=0
        ),
    )(place, activations, *right)


def back_kernel(place, a, i0, i1, i2, i3, mine, other, total):
    accumulate(place, a, (i0, i1, i2, i3), total, None)
    finish(place, total, mine, other)


def back_gram_kernel(place, a, i0, i1, i2, i3, mine, other, gram, total, square):
    accumulate(place, a, (i0, i1, i2, i3), total, square)
    finish(place, total, mine, other)

    @pl.when(pl.program_id(0) == NY - 1)
    def _():
        width = square.shape[1] // NY
        turned = pltpu.roll(square[...], lax.rem((NY - place[0]) * width, NY * width), 1)
        gram[...] = turned[:, : gram.shape[1]]


def accumulate(place, a, images, total, square):
    step = pl.program_id(0)
    for k, image in enumerate(images):
        @pl.when(step == k)
        def _(k=k, image=image):
            part = lax.dot_general(image[...], a[...], FIRST, preferred_element_type=F32)
            total[...] = part if k == 0 else total[...] + part
            if square is not None:
                part = lax.dot_general(image[...], image[...], FIRST, preferred_element_type=F32)
                square[...] = part if k == 0 else square[...] + part


def finish(place, total, mine, other):
    @pl.when(pl.program_id(0) == NY - 1)
    def _():
        half = mine.shape[1]
        mine[...] = total[:, pl.ds(pl.multiple_of(place[1] * half, half), half)]
        there = pl.multiple_of((1 - place[1]) * half, half)
        other[...] = total[:, pl.ds(there, half)].astype(BF16)


def back(place, activations, images, with_gram):
    rows, width = activations.shape
    m, rank = images[0].shape
    half = width // NC
    out_specs = [whole((rank, half)), whole((rank, half))]
    out_shape = [
        jax.ShapeDtypeStruct((rank, half), F32),
        jax.ShapeDtypeStruct((rank, half), BF16),
    ]
    scratch = [pltpu.VMEM((rank, width), F32)]
    if with_gram:
        out_specs.append(whole((rank, 128)))
        out_shape.append(jax.ShapeDtypeStruct((rank, 128), F32))
        scratch.append(pltpu.VMEM((rank, rank), F32))
    return pl.pallas_call(
        back_gram_kernel if with_gram else back_kernel,
        grid_spec=pltpu.PrefetchScalarGridSpec(
            num_scalar_prefetch=1,
            grid=(NY,),
            in_specs=[pl.BlockSpec((m, width), lambda s, place: (lax.rem(place[0] + s, NY), 0))]
            + [whole((m, rank))] * NY,
            out_specs=out_specs,
            scratch_shapes=scratch,
        ),
        out_shape=out_shape,
        compiler_params=PARAMS,
        cost_estimate=pl.CostEstimate(
            flops=2 * rows * width * rank, bytes_accessed=rows * width * 2, transcendentals=0
        ),
    )(place, activations, *images)


def small_inverse(block, block_at):
    rows = lax.broadcasted_iota(jnp.int32, (8, 128), 0)
    e = list(block)
    for group in range(4):
        c = {}
        for j in range(8):
            lane = block_at + 8 * group + j
            for g in range(group, 4):
                c[j, g] = jnp.broadcast_to(e[g][:, lane : lane + 1], (8, 128))
        for k in range(8):
            root = lax.rsqrt(jnp.broadcast_to(c[k, group][k : k + 1, :], (8, 128)))
            col = {g: c[k, g] * root for g in range(group, 4)}
            row = jnp.broadcast_to(e[group][k : k + 1, :], (8, 128)) * root
            below = jnp.where(rows > k, col[group], 0.0)
            for j in range(k + 1, 8):
                times = jnp.broadcast_to(col[group][j : j + 1, :], (8, 128))
                c[j, group] = c[j, group] - below * times
                for g in range(group + 1, 4):
                    c[j, g] = c[j, g] - col[g] * times
            e[group] = jnp.where(rows == k, row, e[group] - below * row)
            for g in range(group + 1, 4):
                e[g] = e[g] - col[g] * row
    return e


def eliminate(m, n):
    lanes = lax.broadcasted_iota(jnp.int32, (8, 128), 1)
    rows = lax.broadcasted_iota(jnp.int32, (8, 128), 0)
    wide = lax.broadcasted_iota(jnp.int32, (32, 128), 1)
    for k0 in range(0, n, 32):
        tile = 128 * (k0 // 128)
        off = k0 - tile
        at = (off + 32) % 128
        groups = []
        for g in range(4):
            v = pltpu.roll(m[k0 + 8 * g : k0 + 8 * g + 8, tile : tile + 128], 32, 1)
            eye = jnp.where(lanes - off == rows + 8 * g, 1.0, 0.0)
            groups.append(jnp.where((lanes >= at) & (lanes < at + 32), v, eye))
        e = jnp.concatenate(small_inverse(groups, at), axis=0)
        e = jnp.where((wide >= off) & (wide < off + 32), e, 0.0)
        lo, hi = (0, n + 128) if k0 < 128 else (128, 2 * n)
        panel = jnp.dot(e, m[tile : tile + 128, lo:hi], precision=EXACT, preferred_element_type=F32)
        m[k0 : k0 + 32, lo:hi] = panel
        done = k0 + 32
        if done < n:
            first = 0 if done < 128 else 128
            left = panel[:, first - lo : n - lo]
            update = lax.dot_general(left, panel, FIRST, precision=EXACT, preferred_element_type=F32)
            m[done:, lo:hi] = m[done:, lo:hi] - update[done - first :]


def inverse_kernel(scale, high, low, out, m):
    n = out.shape[0]
    m[:, :n] = (high[...].astype(F32) + low[...].astype(F32)) * scale
    r = lax.broadcasted_iota(jnp.int32, (n, n), 0)
    c = lax.broadcasted_iota(jnp.int32, (n, n), 1)
    m[:, n:] = jnp.where(r == c, 1.0, 0.0)
    eliminate(m, n)
    out[...] = m[:, n:]


def factor_inverse(gathered, start, scale):
    n = gathered.shape[0]
    at = start // n
    return pl.pallas_call(
        lambda *refs: inverse_kernel(scale, *refs),
        grid=(1,),
        in_specs=[pl.BlockSpec((n, n), lambda s: (0, at)), pl.BlockSpec((n, n), lambda s: (0, at + 1))],
        out_specs=pl.BlockSpec((n, n), lambda s: (0, 0)),
        out_shape=jax.ShapeDtypeStruct((n, n), F32),
        scratch_shapes=[pltpu.VMEM((n, 2 * n), F32)],
        compiler_params=PARAMS,
        cost_estimate=pl.CostEstimate(flops=2 * 10**10, bytes_accessed=2**20, transcendentals=0),
    )(gathered, gathered)


def last_kernel(inverse_root, place, inverse, power, mine, other, basis, projected):
    basis[...] = lax.dot_general(
        power[...], inverse[...], LAST, precision=EXACT, preferred_element_type=F32
    ).astype(BF16)
    scaled = inverse[...] * inverse_root
    high = scaled.astype(BF16)
    low = (scaled - high.astype(F32)).astype(BF16)
    half = other.shape[1]
    for at, value in ((place[1], mine[...]), (1 - place[1], other[...])):
        projected[:, pl.ds(pl.multiple_of(at * half, half), half)] = jnp.dot(
            high, value, preferred_element_type=F32
        ) + jnp.dot(low, value, preferred_element_type=F32)


def last(place, inverse, power, gathered, other, inverse_root):
    m, rank = power.shape
    half = other.shape[1]
    return pl.pallas_call(
        lambda *refs: last_kernel(inverse_root, *refs),
        grid_spec=pltpu.PrefetchScalarGridSpec(
            num_scalar_prefetch=1,
            grid=(1,),
            in_specs=[whole((rank, rank)), whole((m, rank)), whole((rank, half)), whole((rank, half))],
            out_specs=[whole((m, rank)), whole((rank, NC * half))],
        ),
        out_shape=[
            jax.ShapeDtypeStruct((m, rank), BF16),
            jax.ShapeDtypeStruct((rank, NC * half), F32),
        ],
        compiler_params=PARAMS,
    )(place, inverse, power, gathered, other)


def sum_over_y(one, two, three, own):
    got = [from_y(two, 2), from_y(one, 1), from_y(three, 3)]
    return own + got[0].astype(F32) + got[1].astype(F32) + got[2].astype(F32)


def gather_over_y(mine):
    far, on, behind = from_y(mine, 2), from_y(mine, 3), from_y(mine, 1)
    return mine, on, far, behind


def sum_over_plane(value):
    rows, width = value.shape
    got = exchange(value)
    return jnp.sum(got.reshape(PLANE, rows // PLANE, width).astype(F32), axis=0)


def gather_over_plane(mine):
    return exchange(jnp.tile(mine, (PLANE, 1)))


def split(value):
    high = value.astype(BF16)
    return high, (value - high.astype(F32)).astype(BF16)


def per_device(activations, sketch):
    token_count = activations.shape[0] * lax.axis_size("rows")
    rank = sketch.shape[1]
    quarter = rank // NY
    y = lax.axis_index("cols")
    place = jnp.stack([y, lax.axis_index("rows") % NC]).astype(jnp.int32)

    image = sum_over_y(*forward(place, activations, sketch)).astype(BF16)
    mine, other = back(place, activations, gather_over_y(image), False)
    back_image = sum_over_plane((mine + from_core(other).astype(F32)).astype(BF16))
    back_image = gather_over_plane(back_image.astype(BF16))

    power = sum_over_y(*forward(place, activations, back_image, from_core(back_image)))
    mine, other, gram = back(place, activations, gather_over_y(power.astype(BF16)), True)
    mine = (mine + from_core(other).astype(F32)).astype(BF16)
    gram = gram + from_core(gram)
    slab = sum_over_plane(jnp.concatenate([mine, *split(gram[:, :quarter])], axis=1))
    half = mine.shape[1]
    gram = slab[:, half : half + quarter] + slab[:, half + quarter :]
    lanes = lax.broadcasted_iota(jnp.int32, (slab.shape[0], rank), 1)
    gram = jnp.where(lanes // quarter == y, jnp.tile(gram, (1, NY)), 0.0)
    gram = (gram + from_y(gram, 2)) + (from_y(gram, 1) + from_y(gram, 3))
    gathered = gather_over_plane(
        jnp.concatenate([slab[:, :half].astype(BF16), *split(gram)], axis=1)
    )
    other = from_core(gathered[:, :half])
    inverse = factor_inverse(gathered, half, 1.0 / token_count)
    return last(place, inverse, power, gathered, other, 1.0 / math.sqrt(token_count))


def solution(mesh):
    placed = (P("rows", "cols"), P("cols", None))
    return jax.shard_map(
        per_device,
        mesh=mesh,
        in_specs=placed,
        out_specs=(P(("rows", "cols"), None), P(None, "cols")),
        check_vma=False,
    )
```

```python
import functools
import math

import jax
import jax.numpy as jnp
from jax import lax
from jax.experimental import pallas as pl
from jax.experimental.pallas import tpu as pltpu
from jax.sharding import PartitionSpec as P

NZ, NX, NC, NY = 8, 4, 2, 4
PLANE = NZ * NX
F32, BF16 = jnp.float32, jnp.bfloat16
EXACT = lax.Precision.HIGHEST
FIRST = (((0,), (0,)), ((), ()))
LAST = (((1,), (1,)), ((), ()))
PRODUCT = pltpu.CompilerParams(vmem_limit_bytes=16 * 2**20)


def row_index(z, x, c):
    return (z * NX + x) * NC + c


Y_SHIFT = {k: [(i, (i + k) % NY) for i in range(NY)] for k in range(1, NY)}
CORE_SWAP = [(i, i ^ 1) for i in range(NZ * NX * NC)]
PLANES = [[row_index(z, x, c) for z in range(NZ) for x in range(NX)] for c in range(NC)]


def from_y(value, k):
    return lax.ppermute(value, "cols", Y_SHIFT[k])


def from_core(value):
    return lax.ppermute(value, "rows", CORE_SWAP)


def exchange(value):
    return lax.all_to_all(value, "rows", 0, 0, tiled=True, axis_index_groups=PLANES)


VMEM = pl.BlockSpec(memory_space=pltpu.VMEM)
SMEM = pl.BlockSpec(memory_space=pltpu.SMEM)
HBM = pl.BlockSpec(memory_space=pltpu.HBM)


def resident(value):
    return pltpu.with_memory_space_constraint(value, pltpu.VMEM)


def in_hbm(value):
    return pltpu.with_memory_space_constraint(value, pltpu.HBM)


def products(steps, rows, width, rank):
    return pl.CostEstimate(
        flops=2 * steps * rows * width * rank, bytes_accessed=steps * rows * width * 2, transcendentals=0
    )


def load_kernel(quarters, keep_right, place, a, right, *refs):
    count = len(quarters)
    outs, kept, refs = refs[:count], refs[count : 2 * count], refs[2 * count :]
    sems = refs[-1]
    m = outs[0].shape[0]
    copies = []
    if keep_right:
        copies.append(pltpu.make_async_copy(right, refs[0], sems.at[count]))
        right = refs[0]
    for i, k in enumerate(quarters):
        rows = pl.ds(pl.multiple_of(lax.rem(place[0] + k, NY) * m, m), m)
        copies.append(pltpu.make_async_copy(a.at[rows, :], kept[i], sems.at[i]))
    for copy in copies:
        copy.start()
    if keep_right:
        copies.pop(0).wait()
    for i, out in enumerate(outs):
        @pl.when(place[0] >= 0)
        def _(i=i, out=out):
            copies[i].wait()
            part = jnp.dot(kept[i][...], right[...], preferred_element_type=F32)
            out[...] = part.astype(out.dtype)


def load_part(place, activations, right, quarters, types, keep_right):
    rows, width = activations.shape
    count, m, rank = len(quarters), rows // NY, right.shape[1]
    return pl.pallas_call(
        functools.partial(load_kernel, quarters, keep_right),
        in_specs=[SMEM, HBM, HBM if keep_right else VMEM],
        out_specs=[VMEM] * (2 * count + keep_right),
        out_shape=[jax.ShapeDtypeStruct((m, rank), t) for t in types]
        + [pltpu.VMEM((m, width), BF16)] * count
        + [pltpu.VMEM(right.shape, BF16)] * keep_right,
        scratch_shapes=[pltpu.SemaphoreType.DMA((count + keep_right,))],
        compiler_params=PRODUCT,
        cost_estimate=products(count, m, width, rank),
    )(place, in_hbm(activations), (in_hbm if keep_right else resident)(right))


def load_forward(place, activations, right):
    two, one, a2, a1, right = load_part(place, activations, right, (2, 1), (BF16, BF16), True)
    three, own, a3, a0 = load_part(place, activations, right, (3, 0), (BF16, F32), False)
    return (one, two, three, own), (a0, a1, a2, a3)


def forward_kernel(place, mine, other, *refs):
    count = len(refs) // 2
    half = mine.shape[1]
    here = pl.ds(pl.multiple_of(place[1] * half, half), half)
    there = pl.ds(pl.multiple_of((1 - place[1]) * half, half), half)
    for kept, out in zip(refs[:count], refs[count:]):
        part = lax.dot_general(kept[:, here], mine[...], LAST, preferred_element_type=F32)
        part += lax.dot_general(kept[:, there], other[...], LAST, preferred_element_type=F32)
        out[...] = part.astype(out.dtype)


def forward_part(place, kept, mine, other, types):
    m, width = kept[0].shape
    rank = mine.shape[0]
    return pl.pallas_call(
        forward_kernel,
        in_specs=[SMEM] + [VMEM] * (2 + len(kept)),
        out_specs=[VMEM] * len(types),
        out_shape=[jax.ShapeDtypeStruct((m, rank), t) for t in types],
        compiler_params=PRODUCT,
        cost_estimate=products(len(kept), m, width, rank),
    )(place, mine, other, *map(resident, kept))


def forward(place, kept, mine, other):
    two, one = forward_part(place, (kept[2], kept[1]), mine, other, (BF16, BF16))
    three, own = forward_part(place, (kept[3], kept[0]), mine, other, (BF16, F32))
    return one, two, three, own


def back_kernel(count, first, final, with_gram, place, *refs):
    sums = 2 if with_gram else 1
    kept, images, refs = refs[:count], refs[count : 2 * count], refs[2 * count :]
    before = None
    if not first:
        before, refs = refs[:sums], refs[sums:]
    totals = refs[len(refs) - sums :]
    for i, image in enumerate(images):
        value = image[...]
        parts = [lax.dot_general(value, kept[i][...], FIRST, preferred_element_type=F32)]
        if with_gram:
            parts.append(lax.dot_general(value, value, FIRST, preferred_element_type=F32))
        for j, part in enumerate(parts):
            if i > 0:
                part += totals[j][...]
            elif not first:
                part += before[j][...]
            totals[j][...] = part
    if final:
        for j in range(sums):
            total, mine, other = totals[j], refs[2 * j], refs[2 * j + 1]
            half = mine.shape[1]
            mine[...] = total[:, pl.ds(pl.multiple_of(place[1] * half, half), half)]
            there = pl.ds(pl.multiple_of((1 - place[1]) * half, half), half)
            other[...] = total[:, there].astype(other.dtype)


def back_part(place, kept, images, before, final, with_gram):
    m, width = kept[0].shape
    rank = images[0].shape[1]
    sums = [(rank, width)] + ([(rank, rank)] if with_gram else [])
    if final:
        shapes = [
            jax.ShapeDtypeStruct((rank, w // NC), t)
            for (_, w), types in zip(sums, ((F32, BF16), (F32, F32)))
            for t in types
        ]
    else:
        shapes = [pltpu.VMEM(shape, F32) for shape in sums]
    return pl.pallas_call(
        functools.partial(back_kernel, len(images), not before, final, with_gram),
        in_specs=[SMEM] + [VMEM] * (2 * len(images) + len(before)),
        out_specs=[VMEM] * len(shapes),
        out_shape=shapes,
        scratch_shapes=[pltpu.VMEM(shape, F32) for shape in sums] if final else [],
        compiler_params=PRODUCT,
        cost_estimate=products(len(images), m, width, rank),
    )(place, *map(resident, kept), *images, *map(resident, before))


def back(place, kept, images, with_gram):
    own, on, far, behind = images
    total = back_part(place, kept[:1], (own,), (), False, with_gram)
    total = back_part(place, (kept[1], kept[3]), (on, behind), total, False, with_gram)
    return back_part(place, kept[2:3], (far,), total, True, with_gram)


def small_inverse(block, block_at):
    rows = lax.broadcasted_iota(jnp.int32, (8, 128), 0)
    e = list(block)
    for group in range(4):
        c = {}
        for j in range(8):
            lane = block_at + 8 * group + j
            for g in range(group, 4):
                c[j, g] = jnp.broadcast_to(e[g][:, lane : lane + 1], (8, 128))
        for k in range(8):
            root = lax.rsqrt(jnp.broadcast_to(c[k, group][k : k + 1, :], (8, 128)))
            col = {g: c[k, g] * root for g in range(group, 4)}
            row = jnp.broadcast_to(e[group][k : k + 1, :], (8, 128)) * root
            below = jnp.where(rows > k, col[group], 0.0)
            for j in range(k + 1, 8):
                times = jnp.broadcast_to(col[group][j : j + 1, :], (8, 128))
                c[j, group] = c[j, group] - below * times
                for g in range(group + 1, 4):
                    c[j, g] = c[j, g] - col[g] * times
            e[group] = jnp.where(rows == k, row, e[group] - below * row)
            for g in range(group + 1, 4):
                e[g] = e[g] - col[g] * row
    return e


def eliminate(m, n):
    lanes = lax.broadcasted_iota(jnp.int32, (8, 128), 1)
    rows = lax.broadcasted_iota(jnp.int32, (8, 128), 0)
    wide = lax.broadcasted_iota(jnp.int32, (32, 128), 1)
    for k0 in range(0, n, 32):
        tile = 128 * (k0 // 128)
        off = k0 - tile
        at = (off + 32) % 128
        groups = []
        for g in range(4):
            v = pltpu.roll(m[k0 + 8 * g : k0 + 8 * g + 8, tile : tile + 128], 32, 1)
            eye = jnp.where(lanes - off == rows + 8 * g, 1.0, 0.0)
            groups.append(jnp.where((lanes >= at) & (lanes < at + 32), v, eye))
        e = jnp.concatenate(small_inverse(groups, at), axis=0)
        e = jnp.where((wide >= off) & (wide < off + 32), e, 0.0)
        lo, hi = (0, n + 128) if k0 < 128 else (128, 2 * n)
        panel = jnp.dot(e, m[tile : tile + 128, lo:hi], precision=EXACT, preferred_element_type=F32)
        m[k0 : k0 + 32, lo:hi] = panel
        done = k0 + 32
        if done < n:
            first = 0 if done < 128 else 128
            left = panel[:, first - lo : n - lo]
            update = lax.dot_general(left, panel, FIRST, precision=EXACT, preferred_element_type=F32)
            m[done:, lo:hi] = m[done:, lo:hi] - update[done - first :]


def inverse_kernel(scale, start, place, gathered, swapped, out, m):
    n = out.shape[0]
    half = n // NC
    for at, source, first in ((place[1], gathered, start), (1 - place[1], swapped, 0)):
        high = source[:, first : first + half].astype(F32)
        low = source[:, first + half : first + n].astype(F32)
        m[:, pl.ds(pl.multiple_of(at * half, half), half)] = (high + low) * scale
    r = lax.broadcasted_iota(jnp.int32, (n, n), 0)
    c = lax.broadcasted_iota(jnp.int32, (n, n), 1)
    m[:, n:] = jnp.where(r == c, 1.0, 0.0)
    eliminate(m, n)
    out[...] = m[:, n:]


def factor_inverse(place, gathered, start, swapped, scale):
    n = gathered.shape[0]
    return pl.pallas_call(
        functools.partial(inverse_kernel, scale, start),
        in_specs=[SMEM, VMEM, VMEM],
        out_specs=VMEM,
        out_shape=jax.ShapeDtypeStruct((n, n), F32),
        scratch_shapes=[pltpu.VMEM((n, 2 * n), F32)],
        compiler_params=PRODUCT,
        cost_estimate=pl.CostEstimate(flops=10**10, bytes_accessed=2**20, transcendentals=0),
    )(place, gathered, swapped)


def last_kernel(inverse_root, place, inverse, power, gathered, other, basis, projected):
    basis[...] = lax.dot_general(
        power[...], inverse[...], LAST, precision=EXACT, preferred_element_type=F32
    ).astype(BF16)
    scaled = inverse[...] * inverse_root
    high = scaled.astype(BF16)
    low = (scaled - high.astype(F32)).astype(BF16)
    half = other.shape[1]
    for at, source in ((place[1], gathered), (1 - place[1], other)):
        value = source[:, :half]
        projected[:, pl.ds(pl.multiple_of(at * half, half), half)] = jnp.dot(
            high, value, preferred_element_type=F32
        ) + jnp.dot(low, value, preferred_element_type=F32)


def last(place, inverse, power, gathered, other, inverse_root):
    m, rank = power.shape
    return pl.pallas_call(
        functools.partial(last_kernel, inverse_root),
        in_specs=[SMEM] + [VMEM] * 4,
        out_specs=[VMEM] * 2,
        out_shape=[
            jax.ShapeDtypeStruct((m, rank), BF16),
            jax.ShapeDtypeStruct((rank, NC * other.shape[1]), F32),
        ],
        compiler_params=PRODUCT,
    )(place, inverse, power, gathered, other)


def sum_over_y(one, two, three, own):
    got = [from_y(two, 2), from_y(one, 1), from_y(three, 3)]
    return own + got[0].astype(F32) + got[1].astype(F32) + got[2].astype(F32)


def gather_over_y(mine):
    far, on, behind = from_y(mine, 2), from_y(mine, 3), from_y(mine, 1)
    return mine, on, far, behind


def sum_over_plane(value):
    rows, width = value.shape
    got = exchange(value)
    return jnp.sum(got.reshape(PLANE, rows // PLANE, width).astype(F32), axis=0)


def gather_over_plane(mine):
    return exchange(jnp.tile(mine, (PLANE, 1)))


def split(value):
    high = value.astype(BF16)
    return high, (value - high.astype(F32)).astype(BF16)


def per_device(activations, sketch):
    token_count = activations.shape[0] * lax.axis_size("rows")
    place = jnp.stack([lax.axis_index("cols"), lax.axis_index("rows") % NC]).astype(jnp.int32)

    pieces, kept = load_forward(place, activations, sketch)
    image = sum_over_y(*pieces).astype(BF16)
    mine, other = back(place, kept, gather_over_y(image), False)
    back_image = sum_over_plane((mine + from_core(other).astype(F32)).astype(BF16))
    back_image = gather_over_plane(back_image.astype(BF16))

    power = sum_over_y(*forward(place, kept, back_image, from_core(back_image)))
    mine, other, gram, gram_other = back(place, kept, gather_over_y(power.astype(BF16)), True)
    gram = gram + from_core(gram_other)
    mine = (mine + from_core(other).astype(F32)).astype(BF16)
    slab = sum_over_plane(jnp.concatenate([mine, *split(gram)], axis=1))
    half, columns = mine.shape[1], gram.shape[1]
    gram = slab[:, half : half + columns] + slab[:, half + columns :]
    gathered = gather_over_plane(
        jnp.concatenate([slab[:, :half].astype(BF16), *split(gram)], axis=1)
    )
    swapped = from_core(gathered[:, half:])
    inverse = factor_inverse(place, gathered, half, swapped, 1.0 / token_count)
    other = from_core(gathered[:, :half])
    return last(place, inverse, power, gathered, other, 1.0 / math.sqrt(token_count))


def solution(mesh):
    placed = (P("rows", "cols"), P("cols", None))
    return jax.shard_map(
        per_device,
        mesh=mesh,
        in_specs=placed,
        out_specs=(P(("rows", "cols"), None), P(None, "cols")),
        check_vma=False,
    )
```

```python
import functools
import math

import jax
import jax.numpy as jnp
from jax import lax
from jax.experimental import pallas as pl
from jax.experimental.pallas import tpu as pltpu
from jax.sharding import PartitionSpec as P

NZ, NX, NC, NY = 8, 4, 2, 4
PLANE = NZ * NX
F32, BF16 = jnp.float32, jnp.bfloat16
EXACT = lax.Precision.HIGHEST
FIRST = (((0,), (0,)), ((), ()))
LAST = (((1,), (1,)), ((), ()))
PLAIN = (((1,), (0,)), ((), ()))
PRODUCT = pltpu.CompilerParams(vmem_limit_bytes=16 * 2**20)


def row_index(z, x, c):
    return (z * NX + x) * NC + c


Y_SHIFT = {k: [(i, (i + k) % NY) for i in range(NY)] for k in range(1, NY)}
CORE_SWAP = [(i, i ^ 1) for i in range(NZ * NX * NC)]
PLANES = [[row_index(z, x, c) for z in range(NZ) for x in range(NX)] for c in range(NC)]


def from_y(value, k):
    return lax.ppermute(value, "cols", Y_SHIFT[k])


def from_core(value):
    return lax.ppermute(value, "rows", CORE_SWAP)


def exchange(value):
    return lax.all_to_all(value, "rows", 0, 0, tiled=True, axis_index_groups=PLANES)


VMEM = pl.BlockSpec(memory_space=pltpu.VMEM)
SMEM = pl.BlockSpec(memory_space=pltpu.SMEM)
HBM = pl.BlockSpec(memory_space=pltpu.HBM)


def resident(value):
    return pltpu.with_memory_space_constraint(value, pltpu.VMEM)


def in_hbm(value):
    return pltpu.with_memory_space_constraint(value, pltpu.HBM)


def products(steps, rows, width, rank):
    return pl.CostEstimate(
        flops=2 * steps * rows * width * rank, bytes_accessed=steps * rows * width * 2, transcendentals=0
    )


def load_kernel(quarters, keep_right, place, a, right, *refs):
    count = len(quarters)
    outs, kept, refs = refs[:count], refs[count : 2 * count], refs[2 * count :]
    sems = refs[-1]
    m = outs[0].shape[0]
    copies = []
    if keep_right:
        copies.append(pltpu.make_async_copy(right, refs[0], sems.at[count]))
        right = refs[0]
    for i, k in enumerate(quarters):
        rows = pl.ds(pl.multiple_of(lax.rem(place[0] + k, NY) * m, m), m)
        copies.append(pltpu.make_async_copy(a.at[rows, :], kept[i], sems.at[i]))
    for copy in copies:
        copy.start()
    if keep_right:
        copies.pop(0).wait()
    for i, out in enumerate(outs):
        @pl.when(place[0] >= 0)
        def _(i=i, out=out):
            copies[i].wait()
            part = jnp.dot(kept[i][...], right[...], preferred_element_type=F32)
            out[...] = part.astype(out.dtype)


def load_part(place, activations, right, quarters, types, keep_right):
    rows, width = activations.shape
    count, m, rank = len(quarters), rows // NY, right.shape[1]
    return pl.pallas_call(
        functools.partial(load_kernel, quarters, keep_right),
        in_specs=[SMEM, HBM, HBM if keep_right else VMEM],
        out_specs=[VMEM] * (2 * count + keep_right),
        out_shape=[jax.ShapeDtypeStruct((m, rank), t) for t in types]
        + [pltpu.VMEM((m, width), BF16)] * count
        + [pltpu.VMEM(right.shape, BF16)] * keep_right,
        scratch_shapes=[pltpu.SemaphoreType.DMA((count + keep_right,))],
        compiler_params=PRODUCT,
        cost_estimate=products(count, m, width, rank),
    )(place, in_hbm(activations), (in_hbm if keep_right else resident)(right))


def load_forward(place, activations, right):
    two, one, a2, a1, right = load_part(place, activations, right, (2, 1), (BF16, BF16), True)
    three, own, a3, a0 = load_part(place, activations, right, (3, 0), (BF16, F32), False)
    return (one, two, three, own), (a0, a1, a2, a3)


def forward_kernel(side, count, place, image, *refs):
    kept, refs = refs[:count], refs[count:]
    before, outs = refs[: len(refs) - count], refs[len(refs) - count :]
    half = image.shape[1]
    at = (place[1] if side == 0 else 1 - place[1]) * half
    columns = pl.ds(pl.multiple_of(at, half), half)
    for i, out in enumerate(outs):
        part = lax.dot_general(kept[i][:, columns], image[...], LAST, preferred_element_type=F32)
        if before:
            part += before[i][...]
        out[...] = part.astype(out.dtype)


def forward_part(place, kept, image, side, before, types):
    m = kept[0].shape[0]
    rank, half = image.shape
    count = len(kept)
    last = [jax.ShapeDtypeStruct((m, rank), t) for t in types]
    return pl.pallas_call(
        functools.partial(forward_kernel, side, count),
        in_specs=[SMEM] + [VMEM] * (1 + count + len(before)),
        out_specs=[VMEM] * count,
        out_shape=last if before else [pltpu.VMEM((m, rank), t) for t in types],
        compiler_params=PRODUCT,
        cost_estimate=products(count, m, half, rank),
    )(place, image, *map(resident, kept), *map(resident, before))


def forward(place, kept, image):
    parts = forward_part(place, kept, image, 0, (), (F32,) * NY)
    own, one, two, three = forward_part(
        place, kept, from_core(image), 1, parts, (F32, BF16, BF16, BF16)
    )
    return one, two, three, own


def back_kernel(image, kept, out):
    out[...] = lax.dot_general(image[...], kept[...], FIRST, preferred_element_type=F32)


def back_own(kept, image):
    m, width = kept.shape
    rank = image.shape[1]
    return pl.pallas_call(
        back_kernel,
        in_specs=[VMEM] * 2,
        out_specs=VMEM,
        out_shape=pltpu.VMEM((rank, width), F32),
        compiler_params=PRODUCT,
        cost_estimate=products(1, m, width, rank),
    )(image, resident(kept))


def back_half_kernel(side, count, place, before, *refs):
    kept, images, out, total = refs[:count], refs[count : 2 * count], refs[-2], refs[-1]
    half = out.shape[1]
    at = (place[1] if side == 0 else 1 - place[1]) * half
    columns = pl.ds(pl.multiple_of(at, half), half)
    part = before[:, columns]
    for i, image in enumerate(images):
        part += lax.dot_general(image[...], kept[i][:, columns], FIRST, preferred_element_type=F32)
        if i + 1 < count:
            total[...] = part
            part = total[...]
    out[...] = part.astype(out.dtype)


def back_half(place, before, kept, images, side, dtype):
    m, width = kept[0].shape
    rank, half = images[0].shape[1], width // NC
    count = len(images)
    return pl.pallas_call(
        functools.partial(back_half_kernel, side, count),
        in_specs=[SMEM] + [VMEM] * (1 + 2 * count),
        out_specs=VMEM,
        out_shape=jax.ShapeDtypeStruct((rank, half), dtype),
        scratch_shapes=[pltpu.VMEM((rank, half), F32)],
        compiler_params=PRODUCT,
        cost_estimate=products(count, m, half, rank),
    )(place, resident(before), *map(resident, kept), *images)


def back(place, kept, images):
    total = back_own(kept[0], images[0])
    rest = (place, total, (kept[1], kept[3], kept[2]), (images[1], images[3], images[2]))
    other = from_core(back_half(*rest, 1, BF16))
    return (back_half(*rest, 0, F32) + other.astype(F32)).astype(BF16)


def gram_kernel(place, one, two, three, four, mine, other, total):
    for i, image in enumerate((one, two, three, four)):
        value = image[...]
        part = lax.dot_general(value, value, FIRST, preferred_element_type=F32)
        total[...] = part if i == 0 else total[...] + part
    half = mine.shape[1]
    first = place[1] == 0
    mine[...] = jnp.where(first, total[:, :half], total[:, half:])
    other[...] = jnp.where(first, total[:, half:], total[:, :half])


def gram_part(place, images):
    m, rank = images[0].shape
    shape = jax.ShapeDtypeStruct((rank, rank // NC), F32)
    return pl.pallas_call(
        gram_kernel,
        in_specs=[SMEM] + [VMEM] * NY,
        out_specs=[VMEM] * 2,
        out_shape=[shape] * 2,
        scratch_shapes=[pltpu.VMEM((rank, rank), F32)],
        compiler_params=PRODUCT,
        cost_estimate=products(NY, m, rank, rank),
    )(place, *images)


def small_inverse(block, block_at):
    rows = lax.broadcasted_iota(jnp.int32, (8, 128), 0)
    e = list(block)
    groups = len(e)
    for group in range(groups):
        c = {}
        for j in range(8):
            lane = block_at + 8 * group + j
            for g in range(group, groups):
                c[j, g] = jnp.broadcast_to(e[g][:, lane : lane + 1], (8, 128))
        for k in range(8):
            root = lax.rsqrt(jnp.broadcast_to(c[k, group][k : k + 1, :], (8, 128)))
            col = {g: c[k, g] * root for g in range(group, groups)}
            row = jnp.broadcast_to(e[group][k : k + 1, :], (8, 128)) * root
            below = jnp.where(rows > k, col[group], 0.0)
            for j in range(k + 1, 8):
                times = jnp.broadcast_to(col[group][j : j + 1, :], (8, 128))
                c[j, group] = c[j, group] - below * times
                for g in range(group + 1, groups):
                    c[j, g] = c[j, g] - col[g] * times
            e[group] = jnp.where(rows == k, row, e[group] - below * row)
            for g in range(group + 1, groups):
                e[g] = e[g] - col[g] * row
    return e


def invert_block(m):
    n = m.shape[0]
    r = lax.broadcasted_iota(jnp.int32, (n, n), 0)
    c = lax.broadcasted_iota(jnp.int32, (n, n), 1)
    m[:, n:] = jnp.where(r == c, 1.0, 0.0)
    lanes = lax.broadcasted_iota(jnp.int32, (8, n), 1)
    rows = lax.broadcasted_iota(jnp.int32, (8, n), 0)
    size = n // 2
    wide = lax.broadcasted_iota(jnp.int32, (size, n), 1)
    for k0 in range(0, n, size):
        at = (k0 + size) % n
        groups = []
        for g in range(size // 8):
            v = pltpu.roll(m[k0 + 8 * g : k0 + 8 * g + 8, :n], size, 1)
            eye = jnp.where(lanes - k0 == rows + 8 * g, 1.0, 0.0)
            groups.append(jnp.where((lanes >= at) & (lanes < at + size), v, eye))
        e = jnp.concatenate(small_inverse(groups, at), axis=0)
        e = jnp.where((wide >= k0) & (wide < k0 + size), e, 0.0)
        panel = exact(e, m[...], PLAIN)
        m[k0 : k0 + size, :] = panel
        done = k0 + size
        if done < n:
            update = exact(panel[:, :n], panel, FIRST)
            m[done:, :] = m[done:, :] - update[done:]


def exact(a, b, dims):
    return lax.dot_general(a, b, dims, precision=EXACT, preferred_element_type=F32)


def inverse_kernel(scale, start, place, gathered, swapped, out, gram, m):
    n = out.shape[0]
    half = n // NC
    for at, source, first in ((place[1], gathered, start), (1 - place[1], swapped, 0)):
        high = source[:, first : first + half].astype(F32)
        low = source[:, first + half : first + n].astype(F32)
        gram[:, pl.ds(pl.multiple_of(at * half, half), half)] = (high + low) * scale
    m[:, :half] = gram[:half, :half]
    invert_block(m)
    one = m[:, half:]
    cross = exact(one, gram[:half, half:], PLAIN)
    m[:, :half] = gram[half:, half:] - exact(cross, cross, FIRST)
    invert_block(m)
    two = m[:, half:]
    out[:half, :half] = one
    out[:half, half:] = jnp.zeros_like(one)
    out[half:, :half] = -exact(two, exact(cross, one, FIRST), PLAIN)
    out[half:, half:] = two


def factor_inverse(place, gathered, start, swapped, scale):
    n = gathered.shape[0]
    return pl.pallas_call(
        functools.partial(inverse_kernel, scale, start),
        in_specs=[SMEM, VMEM, VMEM],
        out_specs=VMEM,
        out_shape=jax.ShapeDtypeStruct((n, n), F32),
        scratch_shapes=[pltpu.VMEM((n, n), F32), pltpu.VMEM((n // 2, n), F32)],
        compiler_params=PRODUCT,
        cost_estimate=pl.CostEstimate(flops=10**10, bytes_accessed=2**20, transcendentals=0),
    )(place, gathered, swapped)


def halves_product(a, b, dims):
    a, b = split(a), split(b)
    terms = [
        lax.dot_general(x, y, dims, preferred_element_type=F32)
        for x, y in ((a[0], b[0]), (a[0], b[1]), (a[1], b[0]))
    ]
    return terms[0] + (terms[1] + terms[2])


def last_kernel(inverse_root, place, inverse, power, gathered, other, basis, projected, rows, wide, sems):
    half = other.shape[1]
    scaled = inverse[...] * inverse_root
    high = scaled.astype(BF16)
    low = (scaled - high.astype(F32)).astype(BF16)
    copies = []
    for i, (at, source) in enumerate(((place[1], gathered), (1 - place[1], other))):
        columns = pl.ds(pl.multiple_of(at * half, half), half)
        copies.append(pltpu.make_async_copy(wide.at[i], projected.at[:, columns], sems.at[i]))

        @pl.when(place[0] >= 0)
        def _(i=i, source=source):
            value = source[:, :half]
            wide[i] = jnp.dot(high, value, preferred_element_type=F32) + jnp.dot(
                low, value, preferred_element_type=F32
            )
            copies[i].start()

    copies.append(pltpu.make_async_copy(rows, basis, sems.at[2]))
    rows[...] = halves_product(power[...], inverse[...], LAST).astype(BF16)
    copies[2].start()
    for copy in copies:
        copy.wait()


def last(place, inverse, power, gathered, other, inverse_root):
    m, rank = power.shape
    half = other.shape[1]
    return pl.pallas_call(
        functools.partial(last_kernel, inverse_root),
        in_specs=[SMEM] + [VMEM] * 4,
        out_specs=[HBM] * 2,
        out_shape=[
            jax.ShapeDtypeStruct((m, rank), BF16),
            jax.ShapeDtypeStruct((rank, NC * half), F32),
        ],
        scratch_shapes=[
            pltpu.VMEM((m, rank), BF16),
            pltpu.VMEM((NC, rank, half), F32),
            pltpu.SemaphoreType.DMA((3,)),
        ],
        compiler_params=PRODUCT,
    )(place, inverse, power, gathered, other)


def sum_over_y(one, two, three, own):
    got = [from_y(two, 2), from_y(one, 1), from_y(three, 3)]
    return own + got[0].astype(F32) + got[1].astype(F32) + got[2].astype(F32)


def gather_over_y(mine):
    far, on, behind = from_y(mine, 2), from_y(mine, 3), from_y(mine, 1)
    return mine, on, far, behind


def spread_kernel(gram_at, got, out):
    rows = 2 * out.shape[0] // PLANE
    total = None
    for at in range(0, got.shape[0], rows):
        pair = got[at : at + rows, :].astype(F32)
        pair = pair[: rows // 2] + pair[rows // 2 :]
        total = pair if total is None else total + pair
    mine = total.astype(BF16)
    if gram_at:
        columns = (total.shape[1] - gram_at) // 2
        gram = total[:, gram_at : gram_at + columns] + total[:, gram_at + columns :]
        mine = jnp.concatenate([total[:, :gram_at].astype(BF16), *split(gram)], axis=1)
    pair = jnp.concatenate([mine, mine], axis=0)
    for at in range(0, got.shape[0], rows):
        out[at : at + rows, :] = pair


def all_sum_over_plane(value, gram_at=0):
    spread = pl.pallas_call(
        functools.partial(spread_kernel, gram_at),
        in_specs=[VMEM],
        out_specs=VMEM,
        out_shape=jax.ShapeDtypeStruct(value.shape, BF16),
        compiler_params=PRODUCT,
    )(exchange(value))
    return exchange(spread)


def split(value):
    high = value.astype(BF16)
    return high, (value - high.astype(F32)).astype(BF16)


def per_device(activations, sketch):
    token_count = activations.shape[0] * lax.axis_size("rows")
    place = jnp.stack([lax.axis_index("cols"), lax.axis_index("rows") % NC]).astype(jnp.int32)

    pieces, kept = load_forward(place, activations, sketch)
    image = sum_over_y(*pieces).astype(BF16)
    back_image = all_sum_over_plane(back(place, kept, gather_over_y(image)))

    power = sum_over_y(*forward(place, kept, back_image))
    images = gather_over_y(power.astype(BF16))
    wide = back(place, kept, images)
    mine, other = gram_part(place, images)
    gram = mine + from_core(other)
    half = wide.shape[1]
    gathered = all_sum_over_plane(jnp.concatenate([wide, *split(gram)], axis=1), half)
    swapped = from_core(gathered[:, half:])
    inverse = factor_inverse(place, gathered, half, swapped, 1.0 / token_count)
    other = from_core(gathered[:, :half])
    return last(place, inverse, power, gathered, other, 1.0 / math.sqrt(token_count))


def solution(mesh):
    placed = (P("rows", "cols"), P("cols", None))
    return jax.shard_map(
        per_device,
        mesh=mesh,
        in_specs=placed,
        out_specs=(P(("rows", "cols"), None), P(None, "cols")),
        check_vma=False,
    )
```

```python
import functools
import math

import jax
import jax.numpy as jnp
from jax import lax
from jax.experimental import pallas as pl
from jax.experimental.pallas import tpu as pltpu
from jax.sharding import PartitionSpec as P

NZ, NX, NC, NY = 8, 4, 2, 4
PLANE = NZ * NX
F32, BF16 = jnp.float32, jnp.bfloat16
EXACT = lax.Precision.HIGHEST
FIRST = (((0,), (0,)), ((), ()))
LAST = (((1,), (1,)), ((), ()))
PLAIN = (((1,), (0,)), ((), ()))
PRODUCT = pltpu.CompilerParams(vmem_limit_bytes=16 * 2**20)


def row_index(z, x, c):
    return (z * NX + x) * NC + c


Y_SHIFT = {k: [(i, (i + k) % NY) for i in range(NY)] for k in range(1, NY)}
CORE_SWAP = [(i, i ^ 1) for i in range(NZ * NX * NC)]
PLANES = [[row_index(z, x, c) for z in range(NZ) for x in range(NX)] for c in range(NC)]


def from_y(value, k):
    return lax.ppermute(value, "cols", Y_SHIFT[k])


def from_x(value, k):
    to = [(row_index(z, x, c), row_index(z, (x + k) % NX, c)) for z in range(NZ) for x in range(NX) for c in range(NC)]
    return lax.ppermute(value, "rows", to)


COLUMNS = [[row_index(z, x, c) for z in range(NZ)] for x in range(NX) for c in range(NC)]


def exchange_z(value):
    return lax.all_to_all(value, "rows", 0, 0, tiled=True, axis_index_groups=COLUMNS)


def from_core(value):
    return lax.ppermute(value, "rows", CORE_SWAP)


def exchange(value):
    return lax.all_to_all(value, "rows", 0, 0, tiled=True, axis_index_groups=PLANES)


VMEM = pl.BlockSpec(memory_space=pltpu.VMEM)
SMEM = pl.BlockSpec(memory_space=pltpu.SMEM)
HBM = pl.BlockSpec(memory_space=pltpu.HBM)


def resident(value):
    return pltpu.with_memory_space_constraint(value, pltpu.VMEM)


def in_hbm(value):
    return pltpu.with_memory_space_constraint(value, pltpu.HBM)


def products(steps, rows, width, rank):
    return pl.CostEstimate(
        flops=2 * steps * rows * width * rank, bytes_accessed=steps * rows * width * 2, transcendentals=0
    )


def load_kernel(quarters, keep_right, place, a, right, *refs):
    count = len(quarters)
    outs, kept, refs = refs[:count], refs[count : 2 * count], refs[2 * count :]
    sems = refs[-1]
    m = outs[0].shape[0]
    copies = []
    if keep_right:
        copies.append(pltpu.make_async_copy(right, refs[0], sems.at[count]))
        right = refs[0]
    for i, k in enumerate(quarters):
        rows = pl.ds(pl.multiple_of(lax.rem(place[0] + k, NY) * m, m), m)
        copies.append(pltpu.make_async_copy(a.at[rows, :], kept[i], sems.at[i]))
    for copy in copies:
        copy.start()
    if keep_right:
        copies.pop(0).wait()
    for i, out in enumerate(outs):
        @pl.when(place[0] >= 0)
        def _(i=i, out=out):
            copies[i].wait()
            part = jnp.dot(kept[i][...], right[...], preferred_element_type=F32)
            out[...] = part.astype(out.dtype)


def load_part(place, activations, right, quarters, types, keep_right):
    rows, width = activations.shape
    count, m, rank = len(quarters), rows // NY, right.shape[1]
    return pl.pallas_call(
        functools.partial(load_kernel, quarters, keep_right),
        in_specs=[SMEM, HBM, HBM if keep_right else VMEM],
        out_specs=[VMEM] * (2 * count + keep_right),
        out_shape=[jax.ShapeDtypeStruct((m, rank), t) for t in types]
        + [pltpu.VMEM((m, width), BF16)] * count
        + [pltpu.VMEM(right.shape, BF16)] * keep_right,
        scratch_shapes=[pltpu.SemaphoreType.DMA((count + keep_right,))],
        compiler_params=PRODUCT,
        cost_estimate=products(count, m, width, rank),
    )(place, in_hbm(activations), (in_hbm if keep_right else resident)(right))


def load_forward(place, activations, right):
    two, one, a2, a1, right = load_part(place, activations, right, (2, 1), (BF16, BF16), True)
    three, own, a3, a0 = load_part(place, activations, right, (3, 0), (BF16, F32), False)
    return (one, two, three, own), (a0, a1, a2, a3)


def forward_kernel(side, count, place, image, *refs):
    kept, refs = refs[:count], refs[count:]
    before, outs = refs[: len(refs) - count], refs[len(refs) - count :]
    half = image.shape[1]
    at = (place[1] if side == 0 else 1 - place[1]) * half
    columns = pl.ds(pl.multiple_of(at, half), half)
    for i, out in enumerate(outs):
        part = lax.dot_general(kept[i][:, columns], image[...], LAST, preferred_element_type=F32)
        if before:
            part += before[i][...]
        out[...] = part.astype(out.dtype)


def forward_part(place, kept, image, side, before, types):
    m = kept[0].shape[0]
    rank, half = image.shape
    count = len(kept)
    last = [jax.ShapeDtypeStruct((m, rank), t) for t in types]
    return pl.pallas_call(
        functools.partial(forward_kernel, side, count),
        in_specs=[SMEM] + [VMEM] * (1 + count + len(before)),
        out_specs=[VMEM] * count,
        out_shape=last if before else [pltpu.VMEM((m, rank), t) for t in types],
        compiler_params=PRODUCT,
        cost_estimate=products(count, m, half, rank),
    )(place, image, *map(resident, kept), *map(resident, before))


def forward(place, kept, image):
    parts = forward_part(place, kept, image, 0, (), (F32,) * NY)
    own, one, two, three = forward_part(
        place, kept, from_core(image), 1, parts, (F32, BF16, BF16, BF16)
    )
    return one, two, three, own


def back_kernel(image, kept, out):
    out[...] = lax.dot_general(image[...], kept[...], FIRST, preferred_element_type=F32)


def back_own(kept, image):
    m, width = kept.shape
    rank = image.shape[1]
    return pl.pallas_call(
        back_kernel,
        in_specs=[VMEM] * 2,
        out_specs=VMEM,
        out_shape=pltpu.VMEM((rank, width), F32),
        compiler_params=PRODUCT,
        cost_estimate=products(1, m, width, rank),
    )(image, resident(kept))


def back_half_kernel(side, count, place, before, *refs):
    kept, images, out, total = refs[:count], refs[count : 2 * count], refs[-2], refs[-1]
    half = out.shape[1]
    at = (place[1] if side == 0 else 1 - place[1]) * half
    columns = pl.ds(pl.multiple_of(at, half), half)
    part = before[:, columns]
    for i, image in enumerate(images):
        part += lax.dot_general(image[...], kept[i][:, columns], FIRST, preferred_element_type=F32)
        if i + 1 < count:
            total[...] = part
            part = total[...]
    out[...] = part.astype(out.dtype)


def back_half(place, before, kept, images, side, dtype):
    m, width = kept[0].shape
    rank, half = images[0].shape[1], width // NC
    count = len(images)
    return pl.pallas_call(
        functools.partial(back_half_kernel, side, count),
        in_specs=[SMEM] + [VMEM] * (1 + 2 * count),
        out_specs=VMEM,
        out_shape=jax.ShapeDtypeStruct((rank, half), dtype),
        scratch_shapes=[pltpu.VMEM((rank, half), F32)],
        compiler_params=PRODUCT,
        cost_estimate=products(count, m, half, rank),
    )(place, resident(before), *map(resident, kept), *images)


def back(place, kept, images):
    total = back_own(kept[0], images[0])
    rest = (place, total, (kept[1], kept[3], kept[2]), (images[1], images[3], images[2]))
    other = from_core(back_half(*rest, 1, BF16))
    return back_half(*rest, 0, F32), other


def gram_kernel(place, one, two, three, four, mine, other, total):
    for i, image in enumerate((one, two, three, four)):
        value = image[...]
        part = lax.dot_general(value, value, FIRST, preferred_element_type=F32)
        total[...] = part if i == 0 else total[...] + part
    m, half = mine.shape
    rows = pl.ds(pl.multiple_of(place[0] * m, m), m)
    mine[...] = total[rows, pl.ds(pl.multiple_of(place[1] * half, half), half)]
    other[...] = total[rows, pl.ds(pl.multiple_of((1 - place[1]) * half, half), half)]


def gram_part(place, images):
    m, rank = images[0].shape
    shape = jax.ShapeDtypeStruct((rank // NY, rank // NC), F32)
    return pl.pallas_call(
        gram_kernel,
        in_specs=[SMEM] + [VMEM] * NY,
        out_specs=[VMEM] * 2,
        out_shape=[shape] * 2,
        scratch_shapes=[pltpu.VMEM((rank, rank), F32)],
        compiler_params=PRODUCT,
        cost_estimate=products(NY, m, rank, rank),
    )(place, *images)


def small_inverse(block, block_at):
    rows = lax.broadcasted_iota(jnp.int32, (8, 128), 0)
    e = list(block)
    groups = len(e)
    for group in range(groups):
        c = {}
        for j in range(8):
            lane = block_at + 8 * group + j
            for g in range(group, groups):
                c[j, g] = jnp.broadcast_to(e[g][:, lane : lane + 1], (8, 128))
        for k in range(8):
            root = lax.rsqrt(jnp.broadcast_to(c[k, group][k : k + 1, :], (8, 128)))
            col = {g: c[k, g] * root for g in range(group, groups)}
            row = jnp.broadcast_to(e[group][k : k + 1, :], (8, 128)) * root
            below = jnp.where(rows > k, col[group], 0.0)
            for j in range(k + 1, 8):
                times = jnp.broadcast_to(col[group][j : j + 1, :], (8, 128))
                c[j, group] = c[j, group] - below * times
                for g in range(group + 1, groups):
                    c[j, g] = c[j, g] - col[g] * times
            e[group] = jnp.where(rows == k, row, e[group] - below * row)
            for g in range(group + 1, groups):
                e[g] = e[g] - col[g] * row
    return e


def invert_block(m):
    n = m.shape[0]
    r = lax.broadcasted_iota(jnp.int32, (n, n), 0)
    c = lax.broadcasted_iota(jnp.int32, (n, n), 1)
    m[:, n:] = jnp.where(r == c, 1.0, 0.0)
    lanes = lax.broadcasted_iota(jnp.int32, (8, n), 1)
    rows = lax.broadcasted_iota(jnp.int32, (8, n), 0)
    size = n // 2
    wide = lax.broadcasted_iota(jnp.int32, (size, n), 1)
    for k0 in range(0, n, size):
        at = (k0 + size) % n
        groups = []
        for g in range(size // 8):
            v = pltpu.roll(m[k0 + 8 * g : k0 + 8 * g + 8, :n], size, 1)
            eye = jnp.where(lanes - k0 == rows + 8 * g, 1.0, 0.0)
            groups.append(jnp.where((lanes >= at) & (lanes < at + size), v, eye))
        e = jnp.concatenate(small_inverse(groups, at), axis=0)
        e = jnp.where((wide >= k0) & (wide < k0 + size), e, 0.0)
        panel = exact(e, m[...], PLAIN)
        m[k0 : k0 + size, :] = panel
        done = k0 + size
        if done < n:
            update = exact(panel[:, :n], panel, FIRST)
            m[done:, :] = m[done:, :] - update[done:]


def exact(a, b, dims):
    return lax.dot_general(a, b, dims, precision=EXACT, preferred_element_type=F32)


def inverse_kernel(scale, place, own, swapped, out, gram, m):
    n = out.shape[0]
    half, quarter = n // NC, n // NY
    for at, source in ((place[1], own), (1 - place[1], swapped)):
        for k in range(NY):
            rows = pl.ds(pl.multiple_of(lax.rem(place[0] + k, NY) * quarter, quarter), quarter)
            value = source[k * quarter : (k + 1) * quarter, :] * scale
            gram[rows, pl.ds(pl.multiple_of(at * half, half), half)] = value
    m[:, :half] = gram[:half, :half]
    invert_block(m)
    one = m[:, half:]
    cross = exact(one, gram[:half, half:], PLAIN)
    m[:, :half] = gram[half:, half:] - exact(cross, cross, FIRST)
    invert_block(m)
    two = m[:, half:]
    out[:half, :half] = one
    out[:half, half:] = jnp.zeros_like(one)
    out[half:, :half] = -exact(two, exact(cross, one, FIRST), PLAIN)
    out[half:, half:] = two


def factor_inverse(place, own, swapped, scale):
    n = own.shape[0]
    return pl.pallas_call(
        functools.partial(inverse_kernel, scale),
        in_specs=[SMEM, VMEM, VMEM],
        out_specs=VMEM,
        out_shape=jax.ShapeDtypeStruct((n, n), F32),
        scratch_shapes=[pltpu.VMEM((n, n), F32), pltpu.VMEM((n // 2, n), F32)],
        compiler_params=PRODUCT,
        cost_estimate=pl.CostEstimate(flops=10**9, bytes_accessed=2**20, transcendentals=0),
    )(place, own, swapped)


def halves_product(a, b, dims):
    a, b = split(a), split(b)
    terms = [
        lax.dot_general(x, y, dims, preferred_element_type=F32)
        for x, y in ((a[0], b[0]), (a[0], b[1]), (a[1], b[0]))
    ]
    return terms[0] + (terms[1] + terms[2])


def last_kernel(inverse_root, place, inverse, power, gathered, other, basis, projected, rows, wide, sems):
    half = other.shape[1]
    scaled = inverse[...] * inverse_root
    high = scaled.astype(BF16)
    low = (scaled - high.astype(F32)).astype(BF16)
    copies = []
    for i, (at, source) in enumerate(((place[1], gathered), (1 - place[1], other))):
        columns = pl.ds(pl.multiple_of(at * half, half), half)
        copies.append(pltpu.make_async_copy(wide.at[i], projected.at[:, columns], sems.at[i]))

        @pl.when(place[0] >= 0)
        def _(i=i, source=source):
            value = source[:, :half]
            wide[i] = jnp.dot(high, value, preferred_element_type=F32) + jnp.dot(
                low, value, preferred_element_type=F32
            )
            copies[i].start()

    copies.append(pltpu.make_async_copy(rows, basis, sems.at[2]))
    rows[...] = halves_product(power[...], inverse[...], LAST).astype(BF16)
    copies[2].start()
    for copy in copies:
        copy.wait()


def last(place, inverse, power, gathered, other, inverse_root):
    m, rank = power.shape
    half = other.shape[1]
    return pl.pallas_call(
        functools.partial(last_kernel, inverse_root),
        in_specs=[SMEM] + [VMEM] * 4,
        out_specs=[HBM] * 2,
        out_shape=[
            jax.ShapeDtypeStruct((m, rank), BF16),
            jax.ShapeDtypeStruct((rank, NC * half), F32),
        ],
        scratch_shapes=[
            pltpu.VMEM((m, rank), BF16),
            pltpu.VMEM((NC, rank, half), F32),
            pltpu.SemaphoreType.DMA((3,)),
        ],
        compiler_params=PRODUCT,
    )(place, inverse, power, gathered, other)


def sum_over_y(one, two, three, own):
    got = [from_y(two, 2), from_y(one, 1), from_y(three, 3)]
    return own + got[0].astype(F32) + got[1].astype(F32) + got[2].astype(F32)


def gather_over_y(mine):
    far, on, behind = from_y(mine, 2), from_y(mine, 3), from_y(mine, 1)
    return mine, on, far, behind


def piece_sum(got, width):
    total = None
    for at in range(0, got.shape[0], 16):
        pair = got[at : at + 16, :width].astype(F32)
        pair = pair[:8] + pair[8:]
        total = pair if total is None else total + pair
    return total


def spread_to(out, value):
    pair = jnp.concatenate([value, value], axis=0)
    for at in range(0, out.shape[0], 16):
        out[at : at + 16, :] = pair


def spread_kernel(got, out):
    spread_to(out, piece_sum(got, out.shape[1]).astype(BF16))


def all_sum_over_plane(value):
    spread = pl.pallas_call(
        spread_kernel,
        in_specs=[VMEM],
        out_specs=VMEM,
        out_shape=jax.ShapeDtypeStruct(value.shape, BF16),
        compiler_params=PRODUCT,
    )(exchange(value))
    return exchange(spread)


def cut_kernel(place, mine, other, gram, own, one, two, three, total):
    total[...] = mine[...] + other[...].astype(F32)
    width = total.shape[1]
    high, low = split(gram[...])
    own[:, width:] = high.astype(F32) + low.astype(F32)
    for out in (one, two, three):
        out[:, width:] = jnp.concatenate([high, low], axis=1)
    for k, out in enumerate((own, one, two, three)):
        x = lax.rem(place[2] + k, NX)
        for z in range(0, NZ, 2):
            blocks = [
                total[pl.ds(pl.multiple_of(8 * (NX * (z + i) + x), 8), 8), :] for i in range(2)
            ]
            out[8 * z : 8 * z + 16, :width] = jnp.concatenate(blocks, axis=0).astype(out.dtype)


def cut(place, mine, other, gram):
    rows, width = mine.shape
    m, size = gram.shape
    return pl.pallas_call(
        cut_kernel,
        in_specs=[SMEM] + [VMEM] * 3,
        out_specs=[VMEM] * NX,
        out_shape=[jax.ShapeDtypeStruct((m, width + size), F32)]
        + [jax.ShapeDtypeStruct((m, width + 2 * size), BF16)] * (NX - 1),
        scratch_shapes=[pltpu.VMEM((rows, width), F32)],
        compiler_params=PRODUCT,
    )(place, mine, other, gram)


def pack_kernel(width, own, one, two, three, out):
    size = own.shape[1] - width
    pieces = [piece[...].astype(F32) for piece in (one, two, three)]
    total = own[:, :width] + pieces[0][:, :width] + pieces[1][:, :width] + pieces[2][:, :width]
    out[:, :width] = total.astype(BF16)
    grams = [piece[:, width : width + size] + piece[:, width + size :] for piece in pieces]
    gram = (own[:, width:] + grams[1]) + (grams[0] + grams[2])
    flat = jnp.concatenate([gram[8 * i : 8 * i + 8] for i in range(gram.shape[0] // 8)], axis=1)
    flat = jnp.concatenate(split(flat), axis=1)
    flat = jnp.concatenate([flat, flat], axis=0)
    for at in range(0, out.shape[0], 16):
        out[at : at + 16, width:] = flat


def pack(width, own, *pieces):
    rows = own.shape[0]
    size = own.shape[1] - width
    return pl.pallas_call(
        functools.partial(pack_kernel, width),
        in_specs=[VMEM] * NX,
        out_specs=VMEM,
        out_shape=jax.ShapeDtypeStruct((rows, width + 2 * rows // 8 * size), BF16),
        compiler_params=PRODUCT,
    )(own, *pieces)


def unpack_kernel(got, out, gram):
    width, size = out.shape[1], gram.shape[1]
    total = piece_sum(got, got.shape[1])
    spread_to(out, total[:, :width].astype(BF16))
    count = gram.shape[0] // 8
    flat = total[:, width : width + count * size] + total[:, width + count * size :]
    for i in range(count):
        gram[8 * i : 8 * i + 8, :] = flat[:, i * size : (i + 1) * size]


def unpack(got, width, shape):
    return pl.pallas_call(
        unpack_kernel,
        in_specs=[VMEM],
        out_specs=[VMEM] * 2,
        out_shape=[
            jax.ShapeDtypeStruct((8 * PLANE, width), BF16),
            jax.ShapeDtypeStruct(shape, F32),
        ],
        compiler_params=PRODUCT,
    )(got)


def split(value):
    high = value.astype(BF16)
    return high, (value - high.astype(F32)).astype(BF16)


def per_device(activations, sketch):
    token_count = activations.shape[0] * lax.axis_size("rows")
    row = lax.axis_index("rows")
    place = jnp.stack([lax.axis_index("cols"), row % NC, row // NC % NX]).astype(jnp.int32)

    pieces, kept = load_forward(place, activations, sketch)
    image = sum_over_y(*pieces).astype(BF16)
    mine, other = back(place, kept, gather_over_y(image))
    back_image = all_sum_over_plane((mine + other.astype(F32)).astype(BF16))

    power = sum_over_y(*forward(place, kept, back_image))
    images = gather_over_y(power.astype(BF16))
    mine, other = back(place, kept, images)
    gram, gram_other = gram_part(place, images)
    gram = gram + from_core(gram_other)
    own, one, two, three = cut(place, mine, other, gram)
    half = mine.shape[1]
    packed = pack(half, own, from_x(one, 1), from_x(two, 2), from_x(three, 3))
    wide, gram = unpack(exchange_z(packed), half, gram.shape)
    wide = exchange(wide)
    gram = jnp.concatenate([gram, from_y(gram, 3), from_y(gram, 2), from_y(gram, 1)], axis=0)
    inverse = factor_inverse(place, gram, from_core(gram), 1.0 / token_count)
    wide, inverse = lax.optimization_barrier((wide, inverse))
    return last(place, inverse, power, wide, from_core(wide), 1.0 / math.sqrt(token_count))


def solution(mesh):
    placed = (P("rows", "cols"), P("cols", None))
    return jax.shard_map(
        per_device,
        mesh=mesh,
        in_specs=placed,
        out_specs=(P(("rows", "cols"), None), P(None, "cols")),
        check_vma=False,
    )
```

```python
import functools
import math

import jax
import jax.numpy as jnp
from jax import lax
from jax.experimental import pallas as pl
from jax.experimental.pallas import tpu as pltpu
from jax.sharding import PartitionSpec as P

NZ, NX, NC, NY = 8, 4, 2, 4
PLANE = NZ * NX
F32, BF16 = jnp.float32, jnp.bfloat16
EXACT = lax.Precision.HIGHEST
FIRST = (((0,), (0,)), ((), ()))
LAST = (((1,), (1,)), ((), ()))
PLAIN = (((1,), (0,)), ((), ()))
PRODUCT = pltpu.CompilerParams(vmem_limit_bytes=16 * 2**20)


def row_index(z, x, c):
    return (z * NX + x) * NC + c


Y_SHIFT = {k: [(i, (i + k) % NY) for i in range(NY)] for k in range(1, NY)}
CORE_SWAP = [(i, i ^ 1) for i in range(NZ * NX * NC)]
PLANES = [[row_index(z, x, c) for z in range(NZ) for x in range(NX)] for c in range(NC)]


def from_y(value, k):
    return lax.ppermute(value, "cols", Y_SHIFT[k])


def from_x(value, k):
    to = [(row_index(z, x, c), row_index(z, (x + k) % NX, c)) for z in range(NZ) for x in range(NX) for c in range(NC)]
    return lax.ppermute(value, "rows", to)


COLUMNS = [[row_index(z, x, c) for z in range(NZ)] for x in range(NX) for c in range(NC)]


def exchange_z(value):
    return lax.all_to_all(value, "rows", 0, 0, tiled=True, axis_index_groups=COLUMNS)


def from_core(value):
    return lax.ppermute(value, "rows", CORE_SWAP)


def exchange(value):
    return lax.all_to_all(value, "rows", 0, 0, tiled=True, axis_index_groups=PLANES)


VMEM = pl.BlockSpec(memory_space=pltpu.VMEM)
SMEM = pl.BlockSpec(memory_space=pltpu.SMEM)
HBM = pl.BlockSpec(memory_space=pltpu.HBM)


def resident(value):
    return pltpu.with_memory_space_constraint(value, pltpu.VMEM)


def in_hbm(value):
    return pltpu.with_memory_space_constraint(value, pltpu.HBM)


def products(steps, rows, width, rank):
    return pl.CostEstimate(
        flops=2 * steps * rows * width * rank, bytes_accessed=steps * rows * width * 2, transcendentals=0
    )


def load_kernel(quarters, keep_right, place, a, right, *refs):
    count = len(quarters)
    outs, kept, refs = refs[:count], refs[count : 2 * count], refs[2 * count :]
    sems = refs[-1]
    m = outs[0].shape[0]
    copies = []
    if keep_right:
        copies.append(pltpu.make_async_copy(right, refs[0], sems.at[count]))
        right = refs[0]
    for i, k in enumerate(quarters):
        rows = pl.ds(pl.multiple_of(lax.rem(place[0] + k, NY) * m, m), m)
        copies.append(pltpu.make_async_copy(a.at[rows, :], kept[i], sems.at[i]))
    for copy in copies:
        copy.start()
    if keep_right:
        copies.pop(0).wait()
    for i, out in enumerate(outs):
        @pl.when(place[0] >= 0)
        def _(i=i, out=out):
            copies[i].wait()
            part = jnp.dot(kept[i][...], right[...], preferred_element_type=F32)
            out[...] = part.astype(out.dtype)


def load_part(place, activations, right, quarters, types, keep_right):
    rows, width = activations.shape
    count, m, rank = len(quarters), rows // NY, right.shape[1]
    return pl.pallas_call(
        functools.partial(load_kernel, quarters, keep_right),
        in_specs=[SMEM, HBM, HBM if keep_right else VMEM],
        out_specs=[VMEM] * (2 * count + keep_right),
        out_shape=[jax.ShapeDtypeStruct((m, rank), t) for t in types]
        + [pltpu.VMEM((m, width), BF16)] * count
        + [pltpu.VMEM(right.shape, BF16)] * keep_right,
        scratch_shapes=[pltpu.SemaphoreType.DMA((count + keep_right,))],
        compiler_params=PRODUCT,
        cost_estimate=products(count, m, width, rank),
    )(place, in_hbm(activations), (in_hbm if keep_right else resident)(right))


def load_forward(place, activations, right):
    two, one, a2, a1, right = load_part(place, activations, right, (2, 1), (BF16, BF16), True)
    three, own, a3, a0 = load_part(place, activations, right, (3, 0), (BF16, F32), False)
    return (one, two, three, own), (a0, a1, a2, a3)


def forward_kernel(side, count, place, image, *refs):
    kept, refs = refs[:count], refs[count:]
    before, outs = refs[: len(refs) - count], refs[len(refs) - count :]
    half = image.shape[1]
    at = (place[1] if side == 0 else 1 - place[1]) * half
    columns = pl.ds(pl.multiple_of(at, half), half)
    for i, out in enumerate(outs):
        part = lax.dot_general(kept[i][:, columns], image[...], LAST, preferred_element_type=F32)
        if before:
            part += before[i][...]
        out[...] = part.astype(out.dtype)


def forward_part(place, kept, image, side, before, types):
    m = kept[0].shape[0]
    rank, half = image.shape
    count = len(kept)
    last = [jax.ShapeDtypeStruct((m, rank), t) for t in types]
    return pl.pallas_call(
        functools.partial(forward_kernel, side, count),
        in_specs=[SMEM] + [VMEM] * (1 + count + len(before)),
        out_specs=[VMEM] * count,
        out_shape=last if before else [pltpu.VMEM((m, rank), t) for t in types],
        compiler_params=PRODUCT,
        cost_estimate=products(count, m, half, rank),
    )(place, image, *map(resident, kept), *map(resident, before))


def forward(place, kept, image):
    parts = forward_part(place, kept, image, 0, (), (F32,) * NY)
    own, one, two, three = forward_part(
        place, kept, from_core(image), 1, parts, (F32, BF16, BF16, BF16)
    )
    return one, two, three, own


def back_kernel(image, kept, out):
    out[...] = lax.dot_general(image[...], kept[...], FIRST, preferred_element_type=F32)


def back_own(kept, image):
    m, width = kept.shape
    rank = image.shape[1]
    return pl.pallas_call(
        back_kernel,
        in_specs=[VMEM] * 2,
        out_specs=VMEM,
        out_shape=pltpu.VMEM((rank, width), F32),
        compiler_params=PRODUCT,
        cost_estimate=products(1, m, width, rank),
    )(image, resident(kept))


def back_half_kernel(side, count, place, before, *refs):
    kept, images, out, total = refs[:count], refs[count : 2 * count], refs[-2], refs[-1]
    half = out.shape[1]
    at = (place[1] if side == 0 else 1 - place[1]) * half
    columns = pl.ds(pl.multiple_of(at, half), half)
    part = before[:, columns]
    for i, image in enumerate(images):
        part += lax.dot_general(image[...], kept[i][:, columns], FIRST, preferred_element_type=F32)
        if i + 1 < count:
            total[...] = part
            part = total[...]
    out[...] = part.astype(out.dtype)


def back_half(place, before, kept, images, side, dtype):
    m, width = kept[0].shape
    rank, half = images[0].shape[1], width // NC
    count = len(images)
    return pl.pallas_call(
        functools.partial(back_half_kernel, side, count),
        in_specs=[SMEM] + [VMEM] * (1 + 2 * count),
        out_specs=VMEM,
        out_shape=jax.ShapeDtypeStruct((rank, half), dtype),
        scratch_shapes=[pltpu.VMEM((rank, half), F32)],
        compiler_params=PRODUCT,
        cost_estimate=products(count, m, half, rank),
    )(place, resident(before), *map(resident, kept), *images)


def back(place, kept, images):
    total = back_own(kept[0], images[0])
    rest = (place, total, (kept[1], kept[3], kept[2]), (images[1], images[3], images[2]))
    other = from_core(back_half(*rest, 1, BF16))
    return back_half(*rest, 0, F32), other


def gram_kernel(place, one, two, three, four, mine, other, total):
    for i, image in enumerate((one, two, three, four)):
        value = image[...]
        part = lax.dot_general(value, value, FIRST, preferred_element_type=F32)
        total[...] = part if i == 0 else total[...] + part
    m, half = mine.shape
    rows = pl.ds(pl.multiple_of(place[0] * m, m), m)
    mine[...] = total[rows, pl.ds(pl.multiple_of(place[1] * half, half), half)]
    other[...] = total[rows, pl.ds(pl.multiple_of((1 - place[1]) * half, half), half)]


def gram_part(place, images):
    m, rank = images[0].shape
    shape = jax.ShapeDtypeStruct((rank // NY, rank // NC), F32)
    return pl.pallas_call(
        gram_kernel,
        in_specs=[SMEM] + [VMEM] * NY,
        out_specs=[VMEM] * 2,
        out_shape=[shape] * 2,
        scratch_shapes=[pltpu.VMEM((rank, rank), F32)],
        compiler_params=PRODUCT,
        cost_estimate=products(NY, m, rank, rank),
    )(place, *images)


def small_inverse(block, block_at):
    rows = lax.broadcasted_iota(jnp.int32, (8, 128), 0)
    e = list(block)
    groups = len(e)
    for group in range(groups):
        c = {}
        for j in range(8):
            lane = block_at + 8 * group + j
            for g in range(group, groups):
                c[j, g] = jnp.broadcast_to(e[g][:, lane : lane + 1], (8, 128))
        for k in range(8):
            root = lax.rsqrt(jnp.broadcast_to(c[k, group][k : k + 1, :], (8, 128)))
            col = {g: c[k, g] * root for g in range(group, groups)}
            row = jnp.broadcast_to(e[group][k : k + 1, :], (8, 128)) * root
            below = jnp.where(rows > k, col[group], 0.0)
            for j in range(k + 1, 8):
                times = jnp.broadcast_to(col[group][j : j + 1, :], (8, 128))
                c[j, group] = c[j, group] - below * times
                for g in range(group + 1, groups):
                    c[j, g] = c[j, g] - col[g] * times
            e[group] = jnp.where(rows == k, row, e[group] - below * row)
            for g in range(group + 1, groups):
                e[g] = e[g] - col[g] * row
    return e


def invert_block(m):
    n = m.shape[0]
    r = lax.broadcasted_iota(jnp.int32, (n, n), 0)
    c = lax.broadcasted_iota(jnp.int32, (n, n), 1)
    m[:, n:] = jnp.where(r == c, 1.0, 0.0)
    lanes = lax.broadcasted_iota(jnp.int32, (8, n), 1)
    rows = lax.broadcasted_iota(jnp.int32, (8, n), 0)
    size = n // 2
    wide = lax.broadcasted_iota(jnp.int32, (size, n), 1)
    for k0 in range(0, n, size):
        at = (k0 + size) % n
        groups = []
        for g in range(size // 8):
            v = pltpu.roll(m[k0 + 8 * g : k0 + 8 * g + 8, :n], size, 1)
            eye = jnp.where(lanes - k0 == rows + 8 * g, 1.0, 0.0)
            groups.append(jnp.where((lanes >= at) & (lanes < at + size), v, eye))
        e = jnp.concatenate(small_inverse(groups, at), axis=0)
        e = jnp.where((wide >= k0) & (wide < k0 + size), e, 0.0)
        panel = exact(e, m[...], PLAIN)
        m[k0 : k0 + size, :] = panel
        done = k0 + size
        if done < n:
            update = exact(panel[:, :n], panel, FIRST)
            m[done:, :] = m[done:, :] - update[done:]


def exact(a, b, dims):
    return lax.dot_general(a, b, dims, precision=EXACT, preferred_element_type=F32)


def inverse_kernel(scale, place, own, swapped, out, gram, m):
    n = out.shape[0]
    half, quarter = n // NC, n // NY
    for at, source in ((place[1], own), (1 - place[1], swapped)):
        for k in range(NY):
            rows = pl.ds(pl.multiple_of(lax.rem(place[0] + k, NY) * quarter, quarter), quarter)
            value = source[k * quarter : (k + 1) * quarter, :] * scale
            gram[rows, pl.ds(pl.multiple_of(at * half, half), half)] = value
    m[:, :half] = gram[:half, :half]
    invert_block(m)
    one = m[:, half:]
    cross = exact(one, gram[:half, half:], PLAIN)
    m[:, :half] = gram[half:, half:] - exact(cross, cross, FIRST)
    invert_block(m)
    two = m[:, half:]
    out[:half, :half] = one
    out[:half, half:] = jnp.zeros_like(one)
    out[half:, :half] = -exact(two, exact(cross, one, FIRST), PLAIN)
    out[half:, half:] = two


def factor_inverse(place, own, swapped, scale):
    n = own.shape[0]
    return pl.pallas_call(
        functools.partial(inverse_kernel, scale),
        in_specs=[SMEM, VMEM, VMEM],
        out_specs=VMEM,
        out_shape=jax.ShapeDtypeStruct((n, n), F32),
        scratch_shapes=[pltpu.VMEM((n, n), F32), pltpu.VMEM((n // 2, n), F32)],
        compiler_params=PRODUCT,
        cost_estimate=pl.CostEstimate(flops=10**9, bytes_accessed=2**20, transcendentals=0),
    )(place, own, swapped)


def halves_product(a, b, dims):
    a, b = split(a), split(b)
    terms = [
        lax.dot_general(x, y, dims, preferred_element_type=F32)
        for x, y in ((a[0], b[0]), (a[0], b[1]), (a[1], b[0]))
    ]
    return terms[0] + (terms[1] + terms[2])


def project(inverse, inverse_root, value):
    scaled = inverse[...] * inverse_root
    high, low = split(scaled)
    return jnp.dot(high, value, preferred_element_type=F32) + jnp.dot(
        low, value, preferred_element_type=F32
    )


def own_kernel(inverse_root, place, inverse, power, gathered, basis, projected, rows, wide, sems):
    half = gathered.shape[1]
    columns = pl.ds(pl.multiple_of(place[1] * half, half), half)
    wide[...] = project(inverse, inverse_root, gathered[...])
    first = pltpu.make_async_copy(wide, projected.at[:, columns], sems.at[0])
    first.start()
    rows[...] = halves_product(power[...], inverse[...], LAST).astype(BF16)
    second = pltpu.make_async_copy(rows, basis, sems.at[1])
    second.start()
    first.wait()
    second.wait()


def other_kernel(inverse_root, place, inverse, other, before, projected, wide, sems):
    half = other.shape[1]
    columns = pl.ds(pl.multiple_of((1 - place[1]) * half, half), half)
    wide[...] = project(inverse, inverse_root, other[...])
    copy = pltpu.make_async_copy(wide, projected.at[:, columns], sems.at[0])
    copy.start()
    copy.wait()


def last(place, inverse, power, gathered, inverse_root):
    m, rank = power.shape
    half = gathered.shape[1]
    projected = jax.ShapeDtypeStruct((rank, NC * half), F32)
    other = from_core(gathered)
    basis, partly = pl.pallas_call(
        functools.partial(own_kernel, inverse_root),
        in_specs=[SMEM] + [VMEM] * 3,
        out_specs=[HBM] * 2,
        out_shape=[jax.ShapeDtypeStruct((m, rank), BF16), projected],
        scratch_shapes=[
            pltpu.VMEM((m, rank), BF16),
            pltpu.VMEM((rank, half), F32),
            pltpu.SemaphoreType.DMA((2,)),
        ],
        compiler_params=PRODUCT,
        cost_estimate=products(2, rank, half, rank),
    )(place, inverse, power, gathered)
    projected = pl.pallas_call(
        functools.partial(other_kernel, inverse_root),
        in_specs=[SMEM, VMEM, VMEM, HBM],
        out_specs=HBM,
        out_shape=projected,
        scratch_shapes=[pltpu.VMEM((rank, half), F32), pltpu.SemaphoreType.DMA((1,))],
        input_output_aliases={3: 0},
        compiler_params=PRODUCT,
    )(place, inverse, other, partly)
    return basis, projected


def sum_over_y(one, two, three, own):
    got = [from_y(two, 2), from_y(one, 1), from_y(three, 3)]
    return own + got[0].astype(F32) + got[1].astype(F32) + got[2].astype(F32)


def gather_over_y(mine):
    far, on, behind = from_y(mine, 2), from_y(mine, 3), from_y(mine, 1)
    return mine, on, far, behind


def piece_sum(got, width):
    total = None
    for at in range(0, got.shape[0], 16):
        pair = got[at : at + 16, :width].astype(F32)
        pair = pair[:8] + pair[8:]
        total = pair if total is None else total + pair
    return total


def spread_to(out, value):
    pair = jnp.concatenate([value, value], axis=0)
    for at in range(0, out.shape[0], 16):
        out[at : at + 16, :] = pair


def spread_kernel(got, out):
    spread_to(out, piece_sum(got, out.shape[1]).astype(BF16))


def all_sum_over_plane(value):
    spread = pl.pallas_call(
        spread_kernel,
        in_specs=[VMEM],
        out_specs=VMEM,
        out_shape=jax.ShapeDtypeStruct(value.shape, BF16),
        compiler_params=PRODUCT,
    )(exchange(value))
    return exchange(spread)


def cut_kernel(place, mine, other, gram, own, one, two, three, total):
    total[...] = mine[...] + other[...].astype(F32)
    width = total.shape[1]
    high, low = split(gram[...])
    own[:, width:] = high.astype(F32) + low.astype(F32)
    for out in (one, two, three):
        out[:, width:] = jnp.concatenate([high, low], axis=1)
    for k, out in enumerate((own, one, two, three)):
        x = lax.rem(place[2] + k, NX)
        for z in range(0, NZ, 2):
            blocks = [
                total[pl.ds(pl.multiple_of(8 * (NX * (z + i) + x), 8), 8), :] for i in range(2)
            ]
            out[8 * z : 8 * z + 16, :width] = jnp.concatenate(blocks, axis=0).astype(out.dtype)


def cut(place, mine, other, gram):
    rows, width = mine.shape
    m, size = gram.shape
    return pl.pallas_call(
        cut_kernel,
        in_specs=[SMEM] + [VMEM] * 3,
        out_specs=[VMEM] * NX,
        out_shape=[jax.ShapeDtypeStruct((m, width + size), F32)]
        + [jax.ShapeDtypeStruct((m, width + 2 * size), BF16)] * (NX - 1),
        scratch_shapes=[pltpu.VMEM((rows, width), F32)],
        compiler_params=PRODUCT,
    )(place, mine, other, gram)


def pack_kernel(width, own, one, two, three, out):
    size = own.shape[1] - width
    pieces = [piece[...].astype(F32) for piece in (one, two, three)]
    total = own[:, :width] + pieces[0][:, :width] + pieces[1][:, :width] + pieces[2][:, :width]
    out[:, :width] = total.astype(BF16)
    grams = [piece[:, width : width + size] + piece[:, width + size :] for piece in pieces]
    gram = (own[:, width:] + grams[1]) + (grams[0] + grams[2])
    flat = jnp.concatenate([gram[8 * i : 8 * i + 8] for i in range(gram.shape[0] // 8)], axis=1)
    flat = jnp.concatenate(split(flat), axis=1)
    flat = jnp.concatenate([flat, flat], axis=0)
    for at in range(0, out.shape[0], 16):
        out[at : at + 16, width:] = flat


def pack(width, own, *pieces):
    rows = own.shape[0]
    size = own.shape[1] - width
    return pl.pallas_call(
        functools.partial(pack_kernel, width),
        in_specs=[VMEM] * NX,
        out_specs=VMEM,
        out_shape=jax.ShapeDtypeStruct((rows, width + 2 * rows // 8 * size), BF16),
        compiler_params=PRODUCT,
    )(own, *pieces)


def unpack_kernel(got, out, gram):
    width, size = out.shape[1], gram.shape[1]
    total = piece_sum(got, got.shape[1])
    spread_to(out, total[:, :width].astype(BF16))
    count = gram.shape[0] // 8
    flat = total[:, width : width + count * size] + total[:, width + count * size :]
    for i in range(count):
        gram[8 * i : 8 * i + 8, :] = flat[:, i * size : (i + 1) * size]


def unpack(got, width, shape):
    return pl.pallas_call(
        unpack_kernel,
        in_specs=[VMEM],
        out_specs=[VMEM] * 2,
        out_shape=[
            jax.ShapeDtypeStruct((8 * PLANE, width), BF16),
            jax.ShapeDtypeStruct(shape, F32),
        ],
        compiler_params=PRODUCT,
    )(got)


def split(value):
    high = value.astype(BF16)
    return high, (value - high.astype(F32)).astype(BF16)


def per_device(activations, sketch):
    token_count = activations.shape[0] * lax.axis_size("rows")
    row = lax.axis_index("rows")
    place = jnp.stack([lax.axis_index("cols"), row % NC, row // NC % NX]).astype(jnp.int32)

    pieces, kept = load_forward(place, activations, sketch)
    image = sum_over_y(*pieces).astype(BF16)
    mine, other = back(place, kept, gather_over_y(image))
    back_image = all_sum_over_plane((mine + other.astype(F32)).astype(BF16))

    power = sum_over_y(*forward(place, kept, back_image))
    images = gather_over_y(power.astype(BF16))
    mine, other = back(place, kept, images)
    gram, gram_other = gram_part(place, images)
    gram = gram + from_core(gram_other)
    own, one, two, three = cut(place, mine, other, gram)
    half = mine.shape[1]
    packed = pack(half, own, from_x(one, 1), from_x(two, 2), from_x(three, 3))
    wide, gram = unpack(exchange_z(packed), half, gram.shape)
    wide = exchange(wide)
    gram = jnp.concatenate([gram, from_y(gram, 3), from_y(gram, 2), from_y(gram, 1)], axis=0)
    inverse = factor_inverse(place, gram, from_core(gram), 1.0 / token_count)
    wide, inverse = lax.optimization_barrier((wide, inverse))
    return last(place, inverse, power, wide, 1.0 / math.sqrt(token_count))


def solution(mesh):
    placed = (P("rows", "cols"), P("cols", None))
    return jax.shard_map(
        per_device,
        mesh=mesh,
        in_specs=placed,
        out_specs=(P(("rows", "cols"), None), P(None, "cols")),
        check_vma=False,
    )
```
